128 devices in a mesh: gx: 16 (over z, x_lo, core), gy: 4 (over y), vert: 2 (over x_hi).
Axes of the slice: x: 4 (x_hi: 2, x_lo: 2; x = x_hi * 2 + x_lo), y: 4, z: 4, core: 2. Of those that a mesh axis runs over, the one named last changes fastest.
Arguments:
- vectors: bfloat16 [2, 3, 256, 16, 4096], P(None, None, 'vert', 'gx', 'gy'), may hold values from -6 to 6
- links: float32 [2, 2, 3, 3, 16, 4096], P(None, None, None, None, 'gx', 'gy'), may hold values from -4 to 4
- momenta: int32 [2, 3], replicated, may hold values from -2 to 2
- shifts_dir: int32 [3], replicated, may hold values from 0 to 2, each once
Outputs:
- elementals: float32 [256, 2, 3, 2, 256], P(('gx', 'gy'), None, None, None, 'vert')
The draws below stay inside these ranges and needn't reach their ends.
Inputs may be any that keep to these rules, and one draw needn't show every extreme that they name: `momenta`: integer momentum components. `shifts_dir`: each of 0 (no displacement), 1 (one link along +x) and 2 (one link along +y) appears exactly once.
All inputs are finite; a program needn't handle non-finite values.
Results may differ from the reference program's by a relative error of at most 0.0029.
Values may be sent and summed in bfloat16 or wider, within the bound.
A program may use at most 128 MiB of HBM per device.

```python
import math
import jax
import jax.numpy as jnp
from jax import lax

NEV = 256
NZ = 64
NMOM = 2
NDISP = 3
NX = 16
NY = 64


def touch_ends(drawn, key, smallest, high):
    longest = drawn.shape.index(max(drawn.shape))
    spots = []
    for shift in (0, 1):
        where = [jax.random.randint(jax.random.fold_in(key, axis), (), 0, length) for axis, length in enumerate(drawn.shape)]
        where[longest] = (where[longest] + shift) % drawn.shape[longest]
        spots.append(tuple(where))
    return drawn.at[spots[0]].set(smallest).at[spots[1]].set(high)


def shard_levels(key, dims, pieces, smallest, top_value):
    level = 1.0
    for dim, shards_of in pieces:
        heights = jax.random.uniform(jax.random.fold_in(jax.random.fold_in(key, 6), dim), (shards_of,), jnp.float32, smallest / len(pieces), top_value / len(pieces))
        level = level * jnp.repeat(jnp.exp(heights), dims[dim] // shards_of).reshape((-1,) + (1,) * (len(dims) - 1 - dim))
    return level


def centred(own_key, extent, spread, bound, shards=(), kind=jnp.bfloat16):
    loudness = shard_levels(own_key, extent, shards, -0.22, 0.18) if shards else 1.0
    entries = jax.random.normal(own_key, extent, jnp.float32) * spread * loudness
    return jnp.minimum(jnp.maximum(entries, -bound), bound).astype(kind)


def setup_inputs(seed: int = 0) -> dict:
    splits = jax.random.split(jax.random.key(seed), 5)
    vectors = centred(splits[0], (2, 3, NEV, NX, NY * NZ), 1.0, 6.0, ((2, 2), (3, 16), (4, 4)))
    links = centred(splits[1], (2, 2, 3, 3, NX, NY * NZ), 0.6, 4.0, ((4, 16), (5, 4)), jnp.float32)
    momenta = touch_ends(jax.random.randint(splits[2], (NMOM, 3), -2, 3), jax.random.fold_in(splits[2], 1), -2, 2).astype(jnp.int32)
    shifts_dir = jax.random.permutation(splits[3], 3).astype(jnp.int32)
    return {"vectors": vectors, "links": links, "momenta": momenta, "shifts_dir": shifts_dir}


def phase_tables(mom, xpos, ypos, zpos, nx, ny, nz):
    frac_x = jnp.mod(mom[0] * xpos, nx).astype(jnp.float32) / nx
    frac_y = jnp.mod(mom[1] * ypos, ny).astype(jnp.float32) / ny
    frac_z = jnp.mod(mom[2] * zpos, nz).astype(jnp.float32) / nz
    rest = (frac_y[:, None] + frac_z[None, :]).reshape(-1)
    angle = 2.0 * math.pi * (frac_x[:, None] + rest[None, :])
    return (jnp.cos(angle), jnp.sin(angle))

def transport(link, field):
    fre = field[0].astype(jnp.float32)
    fim = field[1].astype(jnp.float32)
    out_re = []
    out_im = []
    for row in range(3):
        acc_re = 0.0
        acc_im = 0.0
        for col in range(3):
            lre = link[0, row, col][None]
            lim = link[1, row, col][None]
            acc_re = acc_re + lre * fre[col] - lim * fim[col]
            acc_im = acc_im + lre * fim[col] + lim * fre[col]
        out_re.append(acc_re)
        out_im.append(acc_im)
    return (jnp.stack(out_re, axis=0), jnp.stack(out_im, axis=0))

def pair_operand(uvr, uvi, cosine, sine):
    wre = (uvr * cosine + uvi * sine).astype(jnp.bfloat16)
    wim = (uvi * cosine - uvr * sine).astype(jnp.bfloat16)
    return (wre, wim)

def reference(vectors, links, momenta, shifts_dir):
    nev = vectors.shape[2]
    xpos_all = jnp.arange(NX, dtype=jnp.int32)
    ypos = jnp.arange(NY, dtype=jnp.int32)
    zpos = jnp.arange(NZ, dtype=jnp.int32)

    def step(total, xi):
        here = lax.dynamic_slice_in_dim(vectors, xi, 1, 3)
        ahead = lax.dynamic_slice_in_dim(vectors, jnp.mod(xi + 1, NX).astype(jnp.int32), 1, 3)
        shaped = here.reshape(2, 3, nev, 1, NY, NZ)
        upward = jnp.roll(shaped, -1, axis=4).reshape(here.shape)
        link_here = lax.dynamic_slice_in_dim(links, xi, 1, 4)
        xpos = lax.dynamic_slice_in_dim(xpos_all, xi, 1, 0)
        left_re = here[0].reshape(3, nev, -1).astype(jnp.float32)
        left_im = here[1].reshape(3, nev, -1).astype(jnp.float32)
        blocks = []
        for m in range(NMOM):
            cosine, sine = phase_tables(momenta[m], xpos, ypos, zpos, NX, NY, NZ)
            row = []
            for k in range(NDISP):
                uvr, uvi = lax.switch(shifts_dir[k], [lambda: (here[0].astype(jnp.float32), here[1].astype(jnp.float32)), lambda: transport(link_here[0], ahead), lambda: transport(link_here[1], upward)])
                wre, wim = pair_operand(uvr, uvi, cosine, sine)
                wre = wre.reshape(3, nev, -1).astype(jnp.float32)
                wim = wim.reshape(3, nev, -1).astype(jnp.float32)

                def prod(a, b):
                    return jnp.einsum('cas,cbs->ab', a, b, precision=lax.Precision.HIGHEST)
                ere = prod(left_re, wre) + prod(left_im, wim)
                eim = prod(left_re, wim) - prod(left_im, wre)
                row.append(jnp.stack([ere, eim], axis=1))
            blocks.append(jnp.stack(row, axis=1))
        return (total + jnp.stack(blocks, axis=1), None)
    start = jnp.zeros((nev, NMOM, NDISP, 2, nev), jnp.float32)
    total, _ = lax.scan(step, start, jnp.arange(NX, dtype=jnp.int32))
    return total * (1.0 / math.sqrt(3.0 * NX * NY * NZ))
```

```python
import math

import jax
import jax.numpy as jnp
from jax import lax
from jax.experimental import pallas as pl
from jax.experimental.pallas import tpu as pltpu
from jax.sharding import PartitionSpec as P

MESH = pl.DeviceIdType.MESH
F32 = jnp.float32
BF16 = jnp.bfloat16

NSUB = 2
U = 128 // NSUB
NT = (((1,), (1,)), ((), ()))
SCALE = 1.0 / math.sqrt(3.0 * 16 * 64 * 64)
PEERS_X = [(d, dc) for d in (2, 1, 3, 0) for dc in (0, 1) if d or dc]


def kernel(
    vec_hbm, links_hbm, mom_ref, dir_ref, out_ref,
    vbuf, lbuf, perm, sbuf, lhs, neg, xh, hs, hr, lsend, ul, ct, st, wt,
    ek, ex, er, sz, rz, sx, rx, oz, ox, sz2, rz2, sx2, rx2, sy, ry, fin,
    vsem, lsem, a_s, a_r, l_s, l_r, xh_s, xh_r, yh_s, yh_r, c_s, c_r,
    z1_s, z1_r, x1_s, x1_r, z2_s, z2_r, x2_s, x2_r, y3_s, y3_r,
):
    gx, gy, hi = lax.axis_index("gx"), lax.axis_index("gy"), lax.axis_index("vert")
    z, lo, c = gx // 4, (gx // 2) % 2, gx % 2
    x = hi * 2 + lo
    e = x * 2 + c
    layer = lo * 2 + c

    def dev(dz=0, dy=0, dx=0, dc=0):
        tx = (x + dx) % 4
        tz = (z + dz) % 4
        tc = (c + dc) % 2
        return (tz * 4 + (tx % 2) * 2 + tc, (gy + dy) % 4, tx // 2)

    def remote(src, dst, s, r, where):
        return pltpu.make_async_remote_copy(
            src_ref=src, dst_ref=dst, send_sem=s, recv_sem=r, device_id=where, device_id_type=MESH
        )

    loads = []
    for u in range(NSUB):
        cp = pltpu.make_async_copy(
            vec_hbm.at[:, pl.ds(u * U, U), :], vbuf.at[:, pl.ds(u * U, U), :], vsem.at[u]
        )
        cp.start()
        loads.append(cp)
    lcopy = pltpu.make_async_copy(links_hbm, lbuf, lsem)
    lcopy.start()

    barrier = pltpu.get_barrier_semaphore()
    peers = [dev(dx=d, dc=dc) for d, dc in PEERS_X]
    peers += [dev(dz=d) for d in (1, 2, 3)] + [dev(dy=d) for d in (1, 2, 3)]
    for p in peers:
        pl.semaphore_signal(barrier, inc=1, device_id=p, device_id_type=MESH)

    site = lax.broadcasted_iota(jnp.int32, (1024, 256), 0)
    col = lax.broadcasted_iota(jnp.int32, (1024, 256), 1)
    core_of = jnp.where(col < 128, c, 1 - c)
    lane = col % 128
    want = (lane // 8) * 64 + lane % 8 + core_of * 8
    for d in range(4):
        q = (x + d) % 4
        perm[d] = jnp.where(site == want + q * 16, 1.0, 0.0).astype(BF16)

    row = lax.broadcasted_iota(jnp.int32, (8, 128), 0)
    ln = lax.broadcasted_iota(jnp.int32, (8, 128), 1)
    first = row < 4
    px = jnp.where(first, mom_ref[0, 0], mom_ref[1, 0])
    py = jnp.where(first, mom_ref[0, 1], mom_ref[1, 1])
    pz = jnp.where(first, mom_ref[0, 2], mom_ref[1, 2])
    turn = (
        4 * ((px * (z * 4 + row % 4)) & 15)
        + ((py * (gy * 16 + ln // 8)) & 63)
        + ((pz * (e * 8 + ln % 8)) & 63)
    )
    angle = (2.0 * math.pi) * (turn.astype(F32) * (1.0 / 64.0))
    ct[...] = jnp.cos(angle)
    st[...] = jnp.sin(angle)

    pl.semaphore_wait(barrier, len(peers))

    def a2a(u, d, dc):
        return remote(
            sbuf.at[d * 2 + dc, :, pl.ds(u * U, U), :],
            lhs.at[pl.ds(layer * 6, 6), hi, pl.ds(u * U, U), :],
            a_s.at[u, d * 2 + dc], a_r.at[u, d * 2 + dc], dev(dx=d, dc=dc),
        )

    def a2a_in(u, d, dc):
        sx_ = (x - d + 4) % 4
        slayer = (sx_ % 2) * 2 + (c + dc) % 2
        return remote(
            sbuf.at[d * 2 + dc, :, pl.ds(u * U, U), :],
            lhs.at[pl.ds(slayer * 6, 6), sx_ // 2, pl.ds(u * U, U), :],
            a_s.at[u, d * 2 + dc], a_r.at[u, d * 2 + dc], dev(dx=d, dc=dc),
        )

    for u in range(NSUB):
        loads[u].wait()
        mine = vbuf[:, u * U:(u + 1) * U, :].reshape(6 * U, 1024)
        for d in (2, 1, 3, 0):
            moved = jnp.dot(mine, perm[d], preferred_element_type=F32).astype(BF16)
            for dc in (0, 1):
                part = moved[:, dc * 128:(dc + 1) * 128].reshape(6, U, 128)
                if d or dc:
                    sbuf[d * 2 + dc, :, u * U:(u + 1) * U, :] = part
                    a2a(u, d, dc).start()
                else:
                    lhs[pl.ds(layer * 6, 6), hi, u * U:(u + 1) * U, :] = part
        if u == 0:
            lcopy.wait()
            rows = [lbuf[pl.ds(t, 36, stride=8), :] for t in range(8)]
            link = jnp.concatenate(rows, axis=1)
            link = jnp.concatenate([link, jnp.zeros((12, 1024), F32)], axis=0)
            part0 = link.astype(BF16)
            rest = link - part0.astype(F32)
            part1 = rest.astype(BF16)
            part2 = (rest - part1.astype(F32)).astype(BF16)
            parts = jnp.concatenate([part0, part1, part2], axis=0)
            for i in range(2):
                slot = 0 if i == 0 else 1 + 2 * lo
                got = jnp.dot(parts, perm[slot], preferred_element_type=F32)
                total = (got[0:48] + got[48:96]) + got[96:144]
                for dc in (0, 1):
                    piece = total[:, dc * 128:(dc + 1) * 128]
                    if i or dc:
                        lsend[i * 2 + dc] = piece
                    else:
                        ul[layer] = piece

    def link_copy(i, dc, slayer):
        tx = hi * 2 + (lo + i) % 2
        return remote(
            lsend.at[i * 2 + dc], ul.at[slayer], l_s.at[i * 2 + dc], l_r.at[i * 2 + dc],
            (z * 4 + (tx % 2) * 2 + (c + dc) % 2, gy, hi),
        )

    LINKS = [(0, 1), (1, 0), (1, 1)]
    for i, dc in LINKS:
        link_copy(i, dc, layer).start()
    for i, dc in LINKS:
        link_copy(i, dc, ((lo + i) % 2) * 2 + (c + dc) % 2).wait_recv()

    lane16 = lax.broadcasted_iota(jnp.int32, (16, 128), 1)

    def transport(l, d, f):
        out = []
        for r in range(3):
            are = aim = None
            for k in range(3):
                ure = ul[l, pl.ds(((d * 2 + 0) * 3 + r) * 3 + k, 1), :]
                uim = ul[l, pl.ds(((d * 2 + 1) * 3 + r) * 3 + k, 1), :]
                tre = ure * f[k] - uim * f[3 + k]
                tim = ure * f[3 + k] + uim * f[k]
                are = tre if are is None else are + tre
                aim = tim if aim is None else aim + tim
            out.append((are, aim))
        return out

    def put(l, d, v, rows, f):
        for m in range(2):
            cs = ct[pl.ds(m * 4 + l, 1), :]
            sn = st[pl.ds(m * 4 + l, 1), :]
            for r in range(3):
                fre, fim = f[r]
                wre = (fre * cs + fim * sn).astype(BF16)
                wim = (fim * cs - fre * sn).astype(BF16)
                wt[m * 3 + d, v, rows, pl.ds((l * 6 + r) * 128, 128)] = wre
                wt[m * 3 + d, v, rows, pl.ds((l * 6 + 3 + r) * 128, 128)] = wim

    def xh_copy(u):
        return remote(
            lhs.at[pl.ds(0, 6), :, pl.ds(u * U, U), :], xh.at[:, :, pl.ds(u * U, U), :],
            xh_s.at[u], xh_r.at[u], dev(dz=3),
        )

    def yh_copy(u):
        return remote(
            hs.at[:, pl.ds(u * U, U), :], hr.at[:, pl.ds(u * U, U), :],
            yh_s.at[u], yh_r.at[u], dev(dy=3),
        )

    CH = U // 16
    for u in range(NSUB):
        for d, dc in PEERS_X:
            a2a_in(u, d, dc).wait_recv()
        xh_copy(u).start()

        def pack(j, carry):
            rows = pl.ds(pl.multiple_of(u * U + j * 16, 16), 16)
            for i in range(6):
                acc = lhs[i, 0, rows, :].astype(F32)
                for s in range(1, 8):
                    v, l = s // 4, s % 4
                    piece = pltpu.roll(lhs[l * 6 + i, v, rows, :].astype(F32), 8 * s, 1)
                    acc = jnp.where(lane16 < 8 * s, acc, piece)
                hs[i, rows, :] = acc.astype(BF16)
            for l in range(4):
                for r in range(3):
                    for v in range(2):
                        neg[l * 3 + r, v, rows, :] = -lhs[l * 6 + 3 + r, v, rows, :]
            return carry

        lax.fori_loop(0, CH, pack, 0)
        yh_copy(u).start()

        def free(j, carry):
            v = j // CH
            rows = pl.ds(pl.multiple_of(u * U + (j % CH) * 16, 16), 16)
            for l in range(4):
                f = [lhs[l * 6 + i, v, rows, :].astype(F32) for i in range(6)]
                put(l, 0, v, rows, [(f[r], f[3 + r]) for r in range(3)])
                if l < 3:
                    f = [lhs[l * 6 + 6 + i, v, rows, :].astype(F32) for i in range(6)]
                    put(l, 1, v, rows, transport(l, 0, f))
            return carry

        lax.fori_loop(0, 2 * CH, free, 0)
        xh_copy(u).wait_recv()
        yh_copy(u).wait_recv()

        def halo(j, carry):
            v = j // CH
            rows = pl.ds(pl.multiple_of(u * U + (j % CH) * 16, 16), 16)
            f = [xh[i, v, rows, :].astype(F32) for i in range(6)]
            put(3, 1, v, rows, transport(3, 0, f))
            for l in range(4):
                f = []
                for i in range(6):
                    here = pltpu.roll(lhs[l * 6 + i, v, rows, :].astype(F32), 120, 1)
                    shift = (248 - 8 * (v * 4 + l)) % 128
                    edge = pltpu.roll(hr[i, rows, :].astype(F32), shift, 1)
                    f.append(jnp.where(lane16 < 120, here, edge))
                put(l, 2, v, rows, transport(l, 1, f))
            return carry

        lax.fori_loop(0, 2 * CH, halo, 0)

    def core_copy(mk):
        return remote(ex.at[mk], er.at[mk], c_s.at[mk], c_r.at[mk], dev(dc=1))

    def products(mk, carry):
        right = wt[mk].reshape(256, 3072)
        re = [lhs[t].reshape(256, 128) for t in range(24)]
        im = []
        for l in range(4):
            im += [neg[l * 3 + r].reshape(256, 128) for r in range(3)]
            im += [lhs[l * 6 + r].reshape(256, 128) for r in range(3)]
        for part, tiles in enumerate((re, im)):
            left = jnp.concatenate(tiles, axis=1)
            prod = lax.dot_general(left, right, NT, preferred_element_type=F32)
            groups = prod.reshape(8, 2, 16, 256)
            even, odd = groups[:, 0], groups[:, 1]
            ek[mk, part] = jnp.where(c == 0, even, odd)
            ex[mk, part] = jnp.where(c == 0, odd, even).astype(BF16)
        core_copy(mk).start()
        return carry

    lax.fori_loop(0, 6, products, 0)

    for mk in range(6):
        core_copy(mk).wait_recv()
        k = mk % 3
        for part in range(2):
            total = ek[mk, part] + er[mk, part].astype(F32)
            if mk < 3:
                ek[mk, part] = total
                for t in range(4):
                    sz[t, k, part] = total[2 * t:2 * t + 2].astype(BF16)
            else:
                ek[mk, part] = total
                four = total.reshape(4, 2, 16, 256)
                for t in range(4):
                    half = four[:, t % 2][:, :, (t // 2) * 128:(t // 2) * 128 + 128]
                    sx[t, k, part] = half.astype(BF16)

    def z1(d):
        return remote(sz.at[(z + d) % 4], rz.at[d - 1], z1_s.at[d - 1], z1_r.at[d - 1], dev(dz=d))

    def x1(d):
        return remote(sx.at[(x + d) % 4], rx.at[d - 1], x1_s.at[d - 1], x1_r.at[d - 1], dev(dx=d))

    for d in (2, 1, 3):
        z1(d).start()
        x1(d).start()
    for d in (1, 3, 2):
        z1(d).wait_recv()
        x1(d).wait_recv()
    for k in range(3):
        for part in range(2):
            total = ek[k, part, pl.ds(z * 2, 2)]
            for d in range(3):
                total = total + rz[d, k, part].astype(F32)
            for t in range(4):
                sx2[t, k, part] = total[t % 2, :, (t // 2) * 128:(t // 2) * 128 + 128]
            lo_part = [ek[3 + k, part, t * 2 + lo, :, pl.ds(pl.multiple_of(hi * 128, 128), 128)] for t in range(4)]
            for t in range(4):
                total = lo_part[t]
                for d in range(3):
                    total = total + rx[d, k, part, t].astype(F32)
                sz2[t, k, part] = total

    def z2(d):
        return remote(sz2.at[(z + d) % 4], rz2.at[d - 1], z2_s.at[d - 1], z2_r.at[d - 1], dev(dz=d))

    def x2(d):
        return remote(sx2.at[(x + d) % 4], rx2.at[d - 1], x2_s.at[d - 1], x2_r.at[d - 1], dev(dx=d))

    for d in (2, 1, 3):
        z2(d).start()
        x2(d).start()
    for d in (1, 3, 2):
        z2(d).wait_recv()
        x2(d).wait_recv()
    for k in range(3):
        for part in range(2):
            one = sx2[x, k, part]
            two = sz2[z, k, part]
            for d in range(3):
                one = one + rx2[d, k, part]
                two = two + rz2[d, k, part]
            for m, total in enumerate((one, two)):
                j = (m * 3 + k) * 2 + part
                for t in range(4):
                    sy[t, pl.ds(j * 4, 4), :] = total[t * 4:t * 4 + 4]

    def y3(d):
        return remote(sy.at[(gy + d) % 4], ry.at[d - 1], y3_s.at[d - 1], y3_r.at[d - 1], dev(dy=d))

    for d in (2, 1, 3):
        y3(d).start()
    for d in (1, 3, 2):
        y3(d).wait_recv()
    fin[...] = (((sy[gy] + ry[0]) + ry[1]) + ry[2]) * SCALE
    for m in range(2):
        for part in range(2):
            by_dir = [fin[pl.ds(((m * 3 + d) * 2 + part) * 4, 4), :] for d in range(3)]
            for k in range(3):
                want_dir = dir_ref[k]
                val = jnp.where(want_dir == 0, by_dir[0], jnp.where(want_dir == 1, by_dir[1], by_dir[2]))
                out_ref[pl.ds((m * 3 + k) * 2 + part, 4, stride=12), :] = val

    for u in range(NSUB):
        for d, dc in PEERS_X:
            a2a(u, d, dc).wait_send()
        xh_copy(u).wait_send()
        yh_copy(u).wait_send()
    for i, dc in LINKS:
        link_copy(i, dc, layer).wait_send()
    for mk in range(6):
        core_copy(mk).wait_send()
    for d in (1, 2, 3):
        z1(d).wait_send()
        x1(d).wait_send()
        z2(d).wait_send()
        x2(d).wait_send()
        y3(d).wait_send()


def per_device(vectors, links, momenta, shifts_dir):
    dma = lambda *n: pltpu.SemaphoreType.DMA(n)
    vm = pltpu.VMEM
    out = pl.pallas_call(
        kernel,
        out_shape=jax.ShapeDtypeStruct((48, 128), F32),
        in_specs=[
            pl.BlockSpec(memory_space=pl.ANY),
            pl.BlockSpec(memory_space=pl.ANY),
            pl.BlockSpec(memory_space=pltpu.SMEM),
            pl.BlockSpec(memory_space=pltpu.SMEM),
        ],
        out_specs=pl.BlockSpec(memory_space=pltpu.VMEM),
        scratch_shapes=[
            vm((6, 128, 1024), BF16),
            vm((288, 128), F32),
            vm((4, 1024, 256), BF16),
            vm((8, 6, 128, 128), BF16),
            vm((24, 2, 128, 128), BF16),
            vm((12, 2, 128, 128), BF16),
            vm((6, 2, 128, 128), BF16),
            vm((6, 128, 128), BF16),
            vm((6, 128, 128), BF16),
            vm((4, 48, 128), F32),
            vm((4, 48, 128), F32),
            vm((8, 128), F32),
            vm((8, 128), F32),
            vm((6, 2, 128, 3072), BF16),
            vm((6, 2, 8, 16, 256), F32),
            vm((6, 2, 8, 16, 256), BF16),
            vm((6, 2, 8, 16, 256), BF16),
            vm((4, 3, 2, 2, 16, 256), BF16),
            vm((3, 3, 2, 2, 16, 256), BF16),
            vm((4, 3, 2, 4, 16, 128), BF16),
            vm((3, 3, 2, 4, 16, 128), BF16),
            vm((8, 128), F32),
            vm((8, 128), F32),
            vm((4, 3, 2, 16, 128), F32),
            vm((3, 3, 2, 16, 128), F32),
            vm((4, 3, 2, 16, 128), F32),
            vm((3, 3, 2, 16, 128), F32),
            vm((4, 48, 128), F32),
            vm((3, 48, 128), F32),
            vm((48, 128), F32),
            dma(NSUB), pltpu.SemaphoreType.DMA,
            dma(NSUB, 8), dma(NSUB, 8), dma(4), dma(4),
            dma(NSUB), dma(NSUB), dma(NSUB), dma(NSUB), dma(6), dma(6),
            dma(3), dma(3), dma(3), dma(3), dma(3), dma(3), dma(3), dma(3), dma(3), dma(3),
        ],
        compiler_params=pltpu.CompilerParams(
            collective_id=0, has_side_effects=True, vmem_limit_bytes=56 * 1024 * 1024
        ),
        name="elementals",
    )(vectors.reshape(6, 128, 1024), links.reshape(288, 128), momenta, shifts_dir)
    return out.reshape(4, 2, 3, 2, 128)


def solution(mesh):
    in_specs = (P(None, None, "vert", "gx", "gy"), P(None, None, None, None, "gx", "gy"), P(), P())
    out_specs = P(("gx", "gy"), None, None, None, "vert")
    return jax.shard_map(
        per_device, mesh=mesh, in_specs=in_specs, out_specs=out_specs, check_vma=False
    )
```

```python
import math

import jax
import jax.numpy as jnp
from jax import lax
from jax.experimental import pallas as pl
from jax.experimental.pallas import tpu as pltpu
from jax.sharding import PartitionSpec as P

MESH = pl.DeviceIdType.MESH
F32 = jnp.float32
BF16 = jnp.bfloat16

NSUB = 4
AHEAD = 2
POINTS = (2, 3)
U = 128 // NSUB
NT = (((1,), (1,)), ((), ()))
SCALE = 1.0 / math.sqrt(3.0 * 16 * 64 * 64)
PEERS_X = [(d, dc) for d in (2, 1, 3, 0) for dc in (0, 1) if d or dc]


def kernel(
    vec_hbm, links_hbm, mom_ref, dir_ref, out_ref,
    vbuf, lbuf, perm, sbuf, lhs, neg, xh, hs, hr, lsend, ul, ct, st, wt,
    ek, ex, er, sz, rz, sx, rx, sz2, rz2, sx2, rx2, sy, ry, fin,
    vsem, lsem, a_s, a_r, l_s, l_r, xh_s, xh_r, yh_s, yh_r, c_s, c_r,
    z1_s, z1_r, x1_s, x1_r, z2_s, z2_r, x2_s, x2_r, y3_s, y3_r,
):
    gx, gy, hi = lax.axis_index("gx"), lax.axis_index("gy"), lax.axis_index("vert")
    z, lo, c = gx // 4, (gx // 2) % 2, gx % 2
    x = hi * 2 + lo
    e = x * 2 + c
    layer = lo * 2 + c

    def dev(dz=0, dy=0, dx=0, dc=0):
        tx = (x + dx) % 4
        tz = (z + dz) % 4
        tc = (c + dc) % 2
        return (tz * 4 + (tx % 2) * 2 + tc, (gy + dy) % 4, tx // 2)

    pending = []

    def go(copy):
        copy.start()
        pending.append(copy)

    def finish():
        for copy in pending:
            copy.wait_send()

    def remote(src, dst, s, r, where):
        return pltpu.make_async_remote_copy(
            src_ref=src, dst_ref=dst, send_sem=s, recv_sem=r, device_id=where, device_id_type=MESH
        )

    loads = []
    for u in range(NSUB):
        cp = pltpu.make_async_copy(
            vec_hbm.at[:, pl.ds(u * U, U), :], vbuf.at[:, pl.ds(u * U, U), :], vsem.at[u]
        )
        cp.start()
        loads.append(cp)
    lcopy = pltpu.make_async_copy(links_hbm, lbuf, lsem)
    lcopy.start()

    barrier = pltpu.get_barrier_semaphore()
    peers = [dev(dx=d, dc=dc) for d, dc in PEERS_X]
    peers += [dev(dz=d) for d in (1, 2, 3)] + [dev(dy=d) for d in (1, 2, 3)]
    for p in peers:
        pl.semaphore_signal(barrier, inc=1, device_id=p, device_id_type=MESH)

    site = lax.broadcasted_iota(jnp.int32, (1024, 256), 0)
    col = lax.broadcasted_iota(jnp.int32, (1024, 256), 1)
    core_of = jnp.where(col < 128, c, 1 - c)
    lane = col % 128
    want = (lane // 8) * 64 + lane % 8 + core_of * 8
    for d in range(4):
        q = (x + d) % 4
        perm[d] = jnp.where(site == want + q * 16, 1.0, 0.0).astype(BF16)

    row = lax.broadcasted_iota(jnp.int32, (8, 128), 0)
    ln = lax.broadcasted_iota(jnp.int32, (8, 128), 1)
    first = row < 4
    px = jnp.where(first, mom_ref[0, 0], mom_ref[1, 0])
    py = jnp.where(first, mom_ref[0, 1], mom_ref[1, 1])
    pz = jnp.where(first, mom_ref[0, 2], mom_ref[1, 2])
    turn = (
        4 * ((px * (z * 4 + row % 4)) & 15)
        + ((py * (gy * 16 + ln // 8)) & 63)
        + ((pz * (e * 8 + ln % 8)) & 63)
    )
    angle = (2.0 * math.pi) * (turn.astype(F32) * (1.0 / 64.0))
    ct[...] = jnp.cos(angle)
    st[...] = jnp.sin(angle)

    pl.semaphore_wait(barrier, len(peers))

    def a2a(u, d, dc):
        return remote(
            sbuf.at[d * 2 + dc, :, pl.ds(u * U, U), :],
            lhs.at[pl.ds(layer * 6, 6), hi, pl.ds(u * U, U), :],
            a_s.at[u, d * 2 + dc], a_r.at[u, d * 2 + dc], dev(dx=d, dc=dc),
        )

    def a2a_in(u, d, dc):
        sx_ = (x - d + 4) % 4
        slayer = (sx_ % 2) * 2 + (c + dc) % 2
        return remote(
            sbuf.at[d * 2 + dc, :, pl.ds(u * U, U), :],
            lhs.at[pl.ds(slayer * 6, 6), sx_ // 2, pl.ds(u * U, U), :],
            a_s.at[u, d * 2 + dc], a_r.at[u, d * 2 + dc], dev(dx=d, dc=dc),
        )

    def move(u):
        loads[u].wait()
        mine = vbuf[:, u * U:(u + 1) * U, :].reshape(6 * U, 1024)
        for d in (2, 1, 3, 0):
            moved = jnp.dot(mine, perm[d], preferred_element_type=F32).astype(BF16)
            for dc in (0, 1):
                part = moved[:, dc * 128:(dc + 1) * 128].reshape(6, U, 128)
                if d or dc:
                    sbuf[d * 2 + dc, :, u * U:(u + 1) * U, :] = part
                else:
                    lhs[pl.ds(layer * 6, 6), hi, u * U:(u + 1) * U, :] = part
                if u < AHEAD and (d or dc):
                    go(a2a(u, d, dc))

    def link_copy(i, dc, slayer):
        tx = hi * 2 + (lo + i) % 2
        return remote(
            lsend.at[i * 2 + dc], ul.at[slayer], l_s.at[i * 2 + dc], l_r.at[i * 2 + dc],
            (z * 4 + (tx % 2) * 2 + (c + dc) % 2, gy, hi),
        )

    LINKS = [(0, 1), (1, 0), (1, 1)]

    def move_links():
        lcopy.wait()
        rows = [lbuf[pl.ds(t, 36, stride=8), :] for t in range(8)]
        link = jnp.concatenate(rows, axis=1)
        link = jnp.concatenate([link, jnp.zeros((12, 1024), F32)], axis=0)
        part0 = link.astype(BF16)
        rest = link - part0.astype(F32)
        part1 = rest.astype(BF16)
        part2 = (rest - part1.astype(F32)).astype(BF16)
        parts = jnp.concatenate([part0, part1, part2], axis=0)
        for i in range(2):
            slot = 0 if i == 0 else 1 + 2 * lo
            got = jnp.dot(parts, perm[slot], preferred_element_type=F32)
            total = (got[0:48] + got[48:96]) + got[96:144]
            for dc in (0, 1):
                piece = total[:, dc * 128:(dc + 1) * 128]
                if i or dc:
                    lsend[i * 2 + dc] = piece
                else:
                    ul[layer] = piece
        for i, dc in LINKS:
            go(link_copy(i, dc, layer))

    move(0)
    move_links()
    for u in range(1, NSUB):
        move(u)
    for i, dc in LINKS:
        link_copy(i, dc, ((lo + i) % 2) * 2 + (c + dc) % 2).wait_recv()

    lane16 = lax.broadcasted_iota(jnp.int32, (16, 128), 1)

    def transport(l, d, f):
        out = []
        for r in range(3):
            are = aim = None
            for k in range(3):
                ure = ul[l, pl.ds(((d * 2 + 0) * 3 + r) * 3 + k, 1), :]
                uim = ul[l, pl.ds(((d * 2 + 1) * 3 + r) * 3 + k, 1), :]
                tre = ure * f[k] - uim * f[3 + k]
                tim = ure * f[3 + k] + uim * f[k]
                are = tre if are is None else are + tre
                aim = tim if aim is None else aim + tim
            out.append((are, aim))
        return out

    def put(l, d, v, u, r0, f):
        for m in range(2):
            cs = ct[pl.ds(m * 4 + l, 1), :]
            sn = st[pl.ds(m * 4 + l, 1), :]
            cols = pl.ds(pl.multiple_of(u * 6 * U + (m * 3 + d) * U + r0, 16), 16)
            for r in range(3):
                fre, fim = f[r]
                wre = (fre * cs + fim * sn).astype(BF16)
                wim = (fim * cs - fre * sn).astype(BF16)
                wt[v, cols, pl.ds((l * 6 + r) * 128, 128)] = wre
                wt[v, cols, pl.ds((l * 6 + 3 + r) * 128, 128)] = wim

    def xh_copy(u):
        return remote(
            lhs.at[pl.ds(0, 6), :, pl.ds(u * U, U), :], xh.at[:, :, pl.ds(u * U, U), :],
            xh_s.at[u], xh_r.at[u], dev(dz=3),
        )

    def yh_copy(u):
        return remote(
            hs.at[:, pl.ds(u * U, U), :], hr.at[:, pl.ds(u * U, U), :],
            yh_s.at[u], yh_r.at[u], dev(dy=3),
        )

    CH = U // 16

    def pack(u):
        def body(j, carry):
            rows = pl.ds(pl.multiple_of(u * U + j * 16, 16), 16)
            for i in range(6):
                acc = lhs[i, 0, rows, :].astype(F32)
                for s in range(1, 8):
                    v, l = s // 4, s % 4
                    piece = pltpu.roll(lhs[l * 6 + i, v, rows, :].astype(F32), 8 * s, 1)
                    acc = jnp.where(lane16 < 8 * s, acc, piece)
                hs[i, rows, :] = acc.astype(BF16)
            for l in range(4):
                for r in range(3):
                    for v in range(2):
                        neg[l * 3 + r, v, rows, :] = -lhs[l * 6 + 3 + r, v, rows, :]
            return carry

        lax.fori_loop(0, CH, body, 0)

    def free(u):
        def body(j, carry):
            v = j // CH
            r0 = (j % CH) * 16
            rows = pl.ds(pl.multiple_of(u * U + r0, 16), 16)
            for l in range(4):
                f = [lhs[l * 6 + i, v, rows, :].astype(F32) for i in range(6)]
                put(l, 0, v, u, r0, [(f[r], f[3 + r]) for r in range(3)])
                if l < 3:
                    f = [lhs[l * 6 + 6 + i, v, rows, :].astype(F32) for i in range(6)]
                    put(l, 1, v, u, r0, transport(l, 0, f))
            return carry

        lax.fori_loop(0, 2 * CH, body, 0)

    def halo(u):
        def body(j, carry):
            v = j // CH
            r0 = (j % CH) * 16
            rows = pl.ds(pl.multiple_of(u * U + r0, 16), 16)
            f = [xh[i, v, rows, :].astype(F32) for i in range(6)]
            put(3, 1, v, u, r0, transport(3, 0, f))
            for l in range(4):
                f = []
                for i in range(6):
                    here = pltpu.roll(lhs[l * 6 + i, v, rows, :].astype(F32), 120, 1)
                    shift = (248 - 8 * (v * 4 + l)) % 128
                    edge = pltpu.roll(hr[i, rows, :].astype(F32), shift, 1)
                    f.append(jnp.where(lane16 < 120, here, edge))
                put(l, 2, v, u, r0, transport(l, 1, f))
            return carry

        lax.fori_loop(0, 2 * CH, body, 0)

    def core_copy(j):
        return remote(ex.at[j], er.at[j], c_s.at[j], c_r.at[j], dev(dc=1))

    def product(j, first, last):
        count = (last - first) * U
        sub = slice(first * U, last * U)
        right = wt[:, pl.ds(pl.multiple_of(j * 128, 128), 128), :].reshape(256, 3072)
        re = [lhs[t, :, sub, :].reshape(2 * count, 128) for t in range(24)]
        im = []
        for l in range(4):
            im += [neg[l * 3 + r, :, sub, :].reshape(2 * count, 128) for r in range(3)]
            im += [lhs[l * 6 + r, :, sub, :].reshape(2 * count, 128) for r in range(3)]
        left = jnp.concatenate([jnp.concatenate(re, axis=1), jnp.concatenate(im, axis=1)], axis=0)
        prod = lax.dot_general(left, right, NT, preferred_element_type=F32)
        groups = prod.reshape(2, 2, count // 32, 2, 16, 256)
        for part in range(2):
            for v in range(2):
                even, odd = groups[part, v, :, 0], groups[part, v, :, 1]
                at = slice(v * 4 + first * U // 32, v * 4 + last * U // 32)
                ek[j, part, at] = jnp.where(c == 0, even, odd)
                ex[j, part, at] = jnp.where(c == 0, odd, even)

    done = 0
    done_cols = 0

    def products(upto):
        nonlocal done, done_cols
        cols = upto * 6 * U // 128
        ends = upto == NSUB

        def old(j, carry):
            product(j, done, upto)
            if ends:
                core_copy(j).start()
            return carry

        def new(j, carry):
            product(j, 0, upto)
            if ends:
                core_copy(j).start()
            return carry

        if done_cols and upto > done:
            lax.fori_loop(0, done_cols, old, 0)
        if cols > done_cols:
            lax.fori_loop(done_cols, cols, new, 0)
        done, done_cols = upto, cols

    for u in range(NSUB):
        for d, dc in PEERS_X:
            a2a_in(u, d, dc).wait_recv()
        if u + AHEAD < NSUB:
            for d, dc in PEERS_X:
                go(a2a(u + AHEAD, d, dc))
        go(xh_copy(u))
        pack(u)
        go(yh_copy(u))
        free(u)
        if u in POINTS:
            products(u)
        xh_copy(u).wait_recv()
        yh_copy(u).wait_recv()
        halo(u)
    products(NSUB)
    pending.extend(core_copy(j) for j in range(6))

    for mk in range(6):
        core_copy(mk).wait_recv()
        k = mk % 3
        for part in range(2):
            total = ek[mk, part] + er[mk, part]
            if mk < 3:
                ek[mk, part] = total
                for t in range(4):
                    sz[t, k, part] = total[2 * t:2 * t + 2].astype(BF16)
            else:
                ek[mk, part] = total
                four = total.reshape(4, 2, 16, 256)
                for t in range(4):
                    half = four[:, t % 2][:, :, (t // 2) * 128:(t // 2) * 128 + 128]
                    sx[t, k, part] = half.astype(BF16)

    def z1(d):
        return remote(sz.at[(z + d) % 4], rz.at[d - 1], z1_s.at[d - 1], z1_r.at[d - 1], dev(dz=d))

    def x1(d):
        return remote(sx.at[(x + d) % 4], rx.at[d - 1], x1_s.at[d - 1], x1_r.at[d - 1], dev(dx=d))

    for d in (2, 1, 3):
        go(z1(d))
        go(x1(d))
    for d in (1, 3, 2):
        z1(d).wait_recv()
        x1(d).wait_recv()
    for k in range(3):
        for part in range(2):
            total = ek[k, part, pl.ds(z * 2, 2)]
            for d in range(3):
                total = total + rz[d, k, part].astype(F32)
            for t in range(4):
                sx2[t, k, part] = total[t % 2, :, (t // 2) * 128:(t // 2) * 128 + 128]
            lo_part = [ek[3 + k, part, t * 2 + lo, :, pl.ds(pl.multiple_of(hi * 128, 128), 128)] for t in range(4)]
            for t in range(4):
                total = lo_part[t]
                for d in range(3):
                    total = total + rx[d, k, part, t].astype(F32)
                sz2[t, k, part] = total

    def z2(d):
        return remote(sz2.at[(z + d) % 4], rz2.at[d - 1], z2_s.at[d - 1], z2_r.at[d - 1], dev(dz=d))

    def x2(d):
        return remote(sx2.at[(x + d) % 4], rx2.at[d - 1], x2_s.at[d - 1], x2_r.at[d - 1], dev(dx=d))

    for d in (2, 1, 3):
        go(z2(d))
        go(x2(d))
    for d in (1, 3, 2):
        z2(d).wait_recv()
        x2(d).wait_recv()
    for k in range(3):
        for part in range(2):
            one = sx2[x, k, part]
            two = sz2[z, k, part]
            for d in range(3):
                one = one + rx2[d, k, part]
                two = two + rz2[d, k, part]
            for m, total in enumerate((one, two)):
                j = (m * 3 + k) * 2 + part
                for t in range(4):
                    sy[t, pl.ds(j * 4, 4), :] = total[t * 4:t * 4 + 4]

    def y3(d):
        return remote(sy.at[(gy + d) % 4], ry.at[d - 1], y3_s.at[d - 1], y3_r.at[d - 1], dev(dy=d))

    for d in (2, 1, 3):
        go(y3(d))
    for d in (1, 3, 2):
        y3(d).wait_recv()
    fin[...] = (((sy[gy] + ry[0]) + ry[1]) + ry[2]) * SCALE
    tiles = [fin[pl.ds(t * 8, 8), :] for t in range(6)]
    lane8 = lax.broadcasted_iota(jnp.int32, (8, 128), 1)

    def natural(mk):
        out = None
        for u in range(NSUB):
            at = u * 6 * U + mk * U
            turned = pltpu.roll(tiles[at // 128], (u * U - at) % 128, 1)
            out = turned if out is None else jnp.where(lane8 < u * U, out, turned)
        return out

    for m in range(2):
        by_dir = [natural(m * 3 + d) for d in range(3)]
        for k in range(3):
            want_dir = dir_ref[k]
            val = jnp.where(want_dir == 0, by_dir[0], jnp.where(want_dir == 1, by_dir[1], by_dir[2]))
            for part in range(2):
                out_ref[pl.ds((m * 3 + k) * 2 + part, 4, stride=12), :] = val[part * 4:part * 4 + 4]

    finish()


def per_device(vectors, links, momenta, shifts_dir):
    dma = lambda *n: pltpu.SemaphoreType.DMA(n)
    vm = pltpu.VMEM
    out = pl.pallas_call(
        kernel,
        out_shape=jax.ShapeDtypeStruct((48, 128), F32),
        in_specs=[
            pl.BlockSpec(memory_space=pl.ANY),
            pl.BlockSpec(memory_space=pl.ANY),
            pl.BlockSpec(memory_space=pltpu.SMEM),
            pl.BlockSpec(memory_space=pltpu.SMEM),
        ],
        out_specs=pl.BlockSpec(memory_space=pltpu.VMEM),
        scratch_shapes=[
            vm((6, 128, 1024), BF16),
            vm((288, 128), F32),
            vm((4, 1024, 256), BF16),
            vm((8, 6, 128, 128), BF16),
            vm((24, 2, 128, 128), BF16),
            vm((12, 2, 128, 128), BF16),
            vm((6, 2, 128, 128), BF16),
            vm((6, 128, 128), BF16),
            vm((6, 128, 128), BF16),
            vm((4, 48, 128), F32),
            vm((4, 48, 128), F32),
            vm((8, 128), F32),
            vm((8, 128), F32),
            vm((2, 768, 3072), BF16),
            vm((6, 2, 8, 16, 256), F32),
            vm((6, 2, 8, 16, 256), F32),
            vm((6, 2, 8, 16, 256), F32),
            vm((4, 3, 2, 2, 16, 256), BF16),
            vm((3, 3, 2, 2, 16, 256), BF16),
            vm((4, 3, 2, 4, 16, 128), BF16),
            vm((3, 3, 2, 4, 16, 128), BF16),
            vm((4, 3, 2, 16, 128), F32),
            vm((3, 3, 2, 16, 128), F32),
            vm((4, 3, 2, 16, 128), F32),
            vm((3, 3, 2, 16, 128), F32),
            vm((4, 48, 128), F32),
            vm((3, 48, 128), F32),
            vm((48, 128), F32),
            dma(NSUB), pltpu.SemaphoreType.DMA,
            dma(NSUB, 8), dma(NSUB, 8), dma(4), dma(4),
            dma(NSUB), dma(NSUB), dma(NSUB), dma(NSUB), dma(6), dma(6),
            dma(3), dma(3), dma(3), dma(3), dma(3), dma(3), dma(3), dma(3), dma(3), dma(3),
        ],
        compiler_params=pltpu.CompilerParams(
            collective_id=0, has_side_effects=True, vmem_limit_bytes=56 * 1024 * 1024
        ),
        name="elementals",
    )(vectors.reshape(6, 128, 1024), links.reshape(288, 128), momenta, shifts_dir)
    return out.reshape(4, 2, 3, 2, 128)


def solution(mesh):
    in_specs = (P(None, None, "vert", "gx", "gy"), P(None, None, None, None, "gx", "gy"), P(), P())
    out_specs = P(("gx", "gy"), None, None, None, "vert")
    return jax.shard_map(
        per_device, mesh=mesh, in_specs=in_specs, out_specs=out_specs, check_vma=False
    )
```

```python
import math

import jax
import jax.numpy as jnp
from jax import lax
from jax.experimental import pallas as pl
from jax.experimental.pallas import tpu as pltpu
from jax.sharding import PartitionSpec as P

MESH = pl.DeviceIdType.MESH
F32 = jnp.float32
BF16 = jnp.bfloat16

NSUB = 4
AHEAD = 2
SPLIT = True
U = 128 // NSUB
NT = (((1,), (1,)), ((), ()))
SCALE = 1.0 / math.sqrt(3.0 * 16 * 64 * 64)
PEERS_X = [(d, dc) for d in (2, 1, 3, 0) for dc in (0, 1) if d or dc]


def kernel(
    vec_hbm, links_hbm, mom_ref, dir_ref, out_ref,
    vbuf, lbuf, perm, sbuf, lhs, neg, xh, hs, hr, lsend, ul, ct, st, wt,
    ek, ex, er, sz_a, rz_a, sx_a, rx_a, sz2_a, rz2_a, sx2_a, rx2_a,
    sz_b, rz_b, sx_b, rx_b, sz2_b, rz2_b, sx2_b, rx2_b, sy, ry, fin,
    vsem, lsem, a_s, a_r, l_s, l_r, xh_s, xh_r, yh_s, yh_r, c_s, c_r,
    z1_s, z1_r, x1_s, x1_r, z2_s, z2_r, x2_s, x2_r, y3_s, y3_r,
):
    gx, gy, hi = lax.axis_index("gx"), lax.axis_index("gy"), lax.axis_index("vert")
    z, lo, c = gx // 4, (gx // 2) % 2, gx % 2
    x = hi * 2 + lo
    e = x * 2 + c
    layer = lo * 2 + c

    def dev(dz=0, dy=0, dx=0, dc=0):
        tx = (x + dx) % 4
        tz = (z + dz) % 4
        tc = (c + dc) % 2
        return (tz * 4 + (tx % 2) * 2 + tc, (gy + dy) % 4, tx // 2)

    pending = []

    def go(copy):
        copy.start()
        pending.append(copy)

    def finish():
        for copy in pending:
            copy.wait_send()

    def remote(src, dst, s, r, where):
        return pltpu.make_async_remote_copy(
            src_ref=src, dst_ref=dst, send_sem=s, recv_sem=r, device_id=where, device_id_type=MESH
        )

    loads = []
    for u in range(NSUB):
        cp = pltpu.make_async_copy(
            vec_hbm.at[:, pl.ds(u * U, U), :], vbuf.at[:, pl.ds(u * U, U), :], vsem.at[u]
        )
        cp.start()
        loads.append(cp)
    lcopy = pltpu.make_async_copy(links_hbm, lbuf, lsem)
    lcopy.start()

    barrier = pltpu.get_barrier_semaphore()
    peers = [dev(dx=d, dc=dc) for d, dc in PEERS_X]
    peers += [dev(dz=d) for d in (1, 2, 3)] + [dev(dy=d) for d in (1, 2, 3)]
    for p in peers:
        pl.semaphore_signal(barrier, inc=1, device_id=p, device_id_type=MESH)

    site = lax.broadcasted_iota(jnp.int32, (1024, 256), 0)
    col = lax.broadcasted_iota(jnp.int32, (1024, 256), 1)
    core_of = jnp.where(col < 128, c, 1 - c)
    lane = col % 128
    want = (lane // 8) * 64 + lane % 8 + core_of * 8
    for d in range(4):
        q = (x + d) % 4
        perm[d] = jnp.where(site == want + q * 16, 1.0, 0.0).astype(BF16)

    row = lax.broadcasted_iota(jnp.int32, (8, 128), 0)
    ln = lax.broadcasted_iota(jnp.int32, (8, 128), 1)
    first = row < 4
    px = jnp.where(first, mom_ref[0, 0], mom_ref[1, 0])
    py = jnp.where(first, mom_ref[0, 1], mom_ref[1, 1])
    pz = jnp.where(first, mom_ref[0, 2], mom_ref[1, 2])
    turn = (
        4 * ((px * (z * 4 + row % 4)) & 15)
        + ((py * (gy * 16 + ln // 8)) & 63)
        + ((pz * (e * 8 + ln % 8)) & 63)
    )
    angle = (2.0 * math.pi) * (turn.astype(F32) * (1.0 / 64.0))
    ct[...] = jnp.cos(angle)
    st[...] = jnp.sin(angle)

    pl.semaphore_wait(barrier, len(peers))

    def a2a(u, d, dc):
        return remote(
            sbuf.at[d * 2 + dc, :, pl.ds(u * U, U), :],
            lhs.at[pl.ds(layer * 6, 6), hi, pl.ds(u * U, U), :],
            a_s.at[u, d * 2 + dc], a_r.at[u, d * 2 + dc], dev(dx=d, dc=dc),
        )

    def a2a_in(u, d, dc):
        sx_ = (x - d + 4) % 4
        slayer = (sx_ % 2) * 2 + (c + dc) % 2
        return remote(
            sbuf.at[d * 2 + dc, :, pl.ds(u * U, U), :],
            lhs.at[pl.ds(slayer * 6, 6), sx_ // 2, pl.ds(u * U, U), :],
            a_s.at[u, d * 2 + dc], a_r.at[u, d * 2 + dc], dev(dx=d, dc=dc),
        )

    def move(u):
        loads[u].wait()
        mine = vbuf[:, u * U:(u + 1) * U, :].reshape(6 * U, 1024)
        for d in (2, 1, 3, 0):
            moved = jnp.dot(mine, perm[d], preferred_element_type=F32).astype(BF16)
            for dc in (0, 1):
                part = moved[:, dc * 128:(dc + 1) * 128].reshape(6, U, 128)
                if d or dc:
                    sbuf[d * 2 + dc, :, u * U:(u + 1) * U, :] = part
                else:
                    lhs[pl.ds(layer * 6, 6), hi, u * U:(u + 1) * U, :] = part
                if u < AHEAD and (d or dc):
                    go(a2a(u, d, dc))

    def link_copy(i, dc, slayer):
        tx = hi * 2 + (lo + i) % 2
        return remote(
            lsend.at[i * 2 + dc], ul.at[slayer], l_s.at[i * 2 + dc], l_r.at[i * 2 + dc],
            (z * 4 + (tx % 2) * 2 + (c + dc) % 2, gy, hi),
        )

    LINKS = [(0, 1), (1, 0), (1, 1)]

    def move_links():
        lcopy.wait()
        rows = [lbuf[pl.ds(t, 36, stride=8), :] for t in range(8)]
        link = jnp.concatenate(rows, axis=1)
        link = jnp.concatenate([link, jnp.zeros((12, 1024), F32)], axis=0)
        part0 = link.astype(BF16)
        rest = link - part0.astype(F32)
        part1 = rest.astype(BF16)
        part2 = (rest - part1.astype(F32)).astype(BF16)
        parts = jnp.concatenate([part0, part1, part2], axis=0)
        for i in range(2):
            slot = 0 if i == 0 else 1 + 2 * lo
            got = jnp.dot(parts, perm[slot], preferred_element_type=F32)
            total = (got[0:48] + got[48:96]) + got[96:144]
            for dc in (0, 1):
                piece = total[:, dc * 128:(dc + 1) * 128]
                if i or dc:
                    lsend[i * 2 + dc] = piece
                else:
                    ul[layer] = piece
        for i, dc in LINKS:
            go(link_copy(i, dc, layer))

    move(0)
    move_links()
    for u in range(1, NSUB):
        move(u)
    for i, dc in LINKS:
        link_copy(i, dc, ((lo + i) % 2) * 2 + (c + dc) % 2).wait_recv()

    lane16 = lax.broadcasted_iota(jnp.int32, (16, 128), 1)

    def transport(l, d, f):
        out = []
        for r in range(3):
            are = aim = None
            for k in range(3):
                ure = ul[l, pl.ds(((d * 2 + 0) * 3 + r) * 3 + k, 1), :]
                uim = ul[l, pl.ds(((d * 2 + 1) * 3 + r) * 3 + k, 1), :]
                tre = ure * f[k] - uim * f[3 + k]
                tim = ure * f[3 + k] + uim * f[k]
                are = tre if are is None else are + tre
                aim = tim if aim is None else aim + tim
            out.append((are, aim))
        return out

    def put(l, d, v, u, r0, f):
        for m in range(2):
            cs = ct[pl.ds(m * 4 + l, 1), :]
            sn = st[pl.ds(m * 4 + l, 1), :]
            cols = pl.ds(pl.multiple_of(u * 6 * U + (m * 3 + d) * U + r0, 16), 16)
            for r in range(3):
                fre, fim = f[r]
                wre = (fre * cs + fim * sn).astype(BF16)
                wim = (fim * cs - fre * sn).astype(BF16)
                wt[v, cols, pl.ds((l * 6 + r) * 128, 128)] = wre
                wt[v, cols, pl.ds((l * 6 + 3 + r) * 128, 128)] = wim

    def xh_copy(u):
        return remote(
            lhs.at[pl.ds(0, 6), :, pl.ds(u * U, U), :], xh.at[:, :, pl.ds(u * U, U), :],
            xh_s.at[u], xh_r.at[u], dev(dz=3),
        )

    def yh_copy(u):
        return remote(
            hs.at[:, pl.ds(u * U, U), :], hr.at[:, pl.ds(u * U, U), :],
            yh_s.at[u], yh_r.at[u], dev(dy=3),
        )

    CH = U // 16

    def pack(u):
        def body(j, carry):
            rows = pl.ds(pl.multiple_of(u * U + j * 16, 16), 16)
            for i in range(6):
                acc = lhs[i, 0, rows, :].astype(F32)
                for s in range(1, 8):
                    v, l = s // 4, s % 4
                    piece = pltpu.roll(lhs[l * 6 + i, v, rows, :].astype(F32), 8 * s, 1)
                    acc = jnp.where(lane16 < 8 * s, acc, piece)
                hs[i, rows, :] = acc.astype(BF16)
            for l in range(4):
                for r in range(3):
                    for v in range(2):
                        neg[l * 3 + r, v, rows, :] = -lhs[l * 6 + 3 + r, v, rows, :]
            return carry

        lax.fori_loop(0, CH, body, 0)

    def free(u):
        def body(j, carry):
            v = j // CH
            r0 = (j % CH) * 16
            rows = pl.ds(pl.multiple_of(u * U + r0, 16), 16)
            for l in range(4):
                f = [lhs[l * 6 + i, v, rows, :].astype(F32) for i in range(6)]
                put(l, 0, v, u, r0, [(f[r], f[3 + r]) for r in range(3)])
                if l < 3:
                    f = [lhs[l * 6 + 6 + i, v, rows, :].astype(F32) for i in range(6)]
                    put(l, 1, v, u, r0, transport(l, 0, f))
            return carry

        lax.fori_loop(0, 2 * CH, body, 0)

    def halo(u):
        def body(j, carry):
            v = j // CH
            r0 = (j % CH) * 16
            rows = pl.ds(pl.multiple_of(u * U + r0, 16), 16)
            f = [xh[i, v, rows, :].astype(F32) for i in range(6)]
            put(3, 1, v, u, r0, transport(3, 0, f))
            for l in range(4):
                f = []
                for i in range(6):
                    here = pltpu.roll(lhs[l * 6 + i, v, rows, :].astype(F32), 120, 1)
                    shift = (248 - 8 * (v * 4 + l)) % 128
                    edge = pltpu.roll(hr[i, rows, :].astype(F32), shift, 1)
                    f.append(jnp.where(lane16 < 120, here, edge))
                put(l, 2, v, u, r0, transport(l, 1, f))
            return carry

        lax.fori_loop(0, 2 * CH, body, 0)

    def core_copy(j):
        return remote(ex.at[j], er.at[j], c_s.at[j], c_r.at[j], dev(dc=1))

    def product(j, first, last):
        count = (last - first) * U
        sub = slice(first * U, last * U)
        right = wt[:, pl.ds(pl.multiple_of(j * 128, 128), 128), :].reshape(256, 3072)
        re = [lhs[t, :, sub, :].reshape(2 * count, 128) for t in range(24)]
        im = []
        for l in range(4):
            im += [neg[l * 3 + r, :, sub, :].reshape(2 * count, 128) for r in range(3)]
            im += [lhs[l * 6 + r, :, sub, :].reshape(2 * count, 128) for r in range(3)]
        left = jnp.concatenate([jnp.concatenate(re, axis=1), jnp.concatenate(im, axis=1)], axis=0)
        prod = lax.dot_general(left, right, NT, preferred_element_type=F32)
        groups = prod.reshape(2, 2, count // 32, 2, 16, 256)
        for part in range(2):
            for v in range(2):
                even, odd = groups[part, v, :, 0], groups[part, v, :, 1]
                at = slice(v * 4 + first * U // 32, v * 4 + last * U // 32)
                ek[j, part, at] = jnp.where(c == 0, even, odd)
                ex[j, part, at] = jnp.where(c == 0, odd, even)

    done_rows = 0
    done_cols = 0

    def products(rows, cols):
        nonlocal done_rows, done_cols
        ends = rows == NSUB
        first = done_rows

        def old(j, carry):
            product(j, first, rows)
            if ends:
                core_copy(j).start()
            return carry

        def new(j, carry):
            product(j, 0, rows)
            if ends:
                core_copy(j).start()
            return carry

        if done_cols and rows > done_rows:
            lax.fori_loop(0, done_cols, old, 0)
        if cols > done_cols:
            lax.fori_loop(done_cols, cols, new, 0)
        done_rows, done_cols = rows, cols

    class Group:
        def __init__(self, n, jz, jx, refs):
            self.n, self.jz, self.jx = n, jz, jx
            (self.sz, self.rz, self.sx, self.rx, self.sz2, self.rz2, self.sx2, self.rx2) = refs

        def z1(self, d):
            n = self.n
            return remote(self.sz.at[(z + d) % 4], self.rz.at[d - 1], z1_s.at[n, d - 1], z1_r.at[n, d - 1], dev(dz=d))

        def x1(self, d):
            n = self.n
            return remote(self.sx.at[(x + d) % 4], self.rx.at[d - 1], x1_s.at[n, d - 1], x1_r.at[n, d - 1], dev(dx=d))

        def z2(self, d):
            n = self.n
            return remote(self.sz2.at[(z + d) % 4], self.rz2.at[d - 1], z2_s.at[n, d - 1], z2_r.at[n, d - 1], dev(dz=d))

        def x2(self, d):
            n = self.n
            return remote(self.sx2.at[(x + d) % 4], self.rx2.at[d - 1], x2_s.at[n, d - 1], x2_r.at[n, d - 1], dev(dx=d))

        def first(self):
            for j in self.jz + self.jx:
                core_copy(j).wait_recv()
            for k, j in enumerate(self.jz):
                for part in range(2):
                    total = ek[j, part] + er[j, part]
                    ek[j, part] = total
                    for t in range(4):
                        self.sz[t, k, part] = total[2 * t:2 * t + 2].astype(BF16)
            for d in (2, 1, 3):
                go(self.z1(d))
            for k, j in enumerate(self.jx):
                for part in range(2):
                    total = ek[j, part] + er[j, part]
                    ek[j, part] = total
                    four = total.reshape(4, 2, 16, 256)
                    for t in range(4):
                        half = four[:, t % 2][:, :, (t // 2) * 128:(t // 2) * 128 + 128]
                        self.sx[t, k, part] = half.astype(BF16)
            for d in (2, 1, 3):
                go(self.x1(d))

        def second(self):
            for d in (1, 3, 2):
                self.z1(d).wait_recv()
            for k, j in enumerate(self.jz):
                for part in range(2):
                    total = ek[j, part, pl.ds(z * 2, 2)]
                    for d in range(3):
                        total = total + self.rz[d, k, part].astype(F32)
                    for t in range(4):
                        self.sx2[t, k, part] = total[t % 2, :, (t // 2) * 128:(t // 2) * 128 + 128]
            for d in (2, 1, 3):
                go(self.x2(d))
            for d in (1, 3, 2):
                self.x1(d).wait_recv()
            for k, j in enumerate(self.jx):
                for part in range(2):
                    for t in range(4):
                        total = ek[j, part, t * 2 + lo, :, pl.ds(pl.multiple_of(hi * 128, 128), 128)]
                        for d in range(3):
                            total = total + self.rx[d, k, part, t].astype(F32)
                        self.sz2[t, k, part] = total
            for d in (2, 1, 3):
                go(self.z2(d))

        def third(self):
            for js, own, sent, got, copy in (
                (self.jz, x, self.sx2, self.rx2, self.x2), (self.jx, z, self.sz2, self.rz2, self.z2)
            ):
                for d in (1, 3, 2):
                    copy(d).wait_recv()
                for k, j in enumerate(js):
                    for part in range(2):
                        total = sent[own, k, part]
                        for d in range(3):
                            total = total + got[d, k, part]
                        for t in range(4):
                            sy[t, pl.ds((j * 2 + part) * 4, 4), :] = total[t * 4:t * 4 + 4]

    early = Group(0, (0, 1), (2, 3), (sz_a, rz_a, sx_a, rx_a, sz2_a, rz2_a, sx2_a, rx2_a))
    late = Group(1, (4,), (5,), (sz_b, rz_b, sx_b, rx_b, sz2_b, rz2_b, sx2_b, rx2_b))

    for u in range(NSUB):
        for d, dc in PEERS_X:
            a2a_in(u, d, dc).wait_recv()
        if u + AHEAD < NSUB:
            for d, dc in PEERS_X:
                go(a2a(u + AHEAD, d, dc))
        go(xh_copy(u))
        pack(u)
        go(yh_copy(u))
        free(u)
        if u:
            xh_copy(u - 1).wait_recv()
            yh_copy(u - 1).wait_recv()
            halo(u - 1)
        if u == 2:
            products(2, 3)
        if u == 3:
            products(4, 4)
    xh_copy(NSUB - 1).wait_recv()
    yh_copy(NSUB - 1).wait_recv()
    halo(NSUB - 1)
    if SPLIT:
        early.first()
        products(4, 6)
    else:
        products(4, 6)
        early.first()
    early.second()
    late.first()
    early.third()
    late.second()
    late.third()
    pending.extend(core_copy(j) for j in range(6))

    def y3(d):
        return remote(sy.at[(gy + d) % 4], ry.at[d - 1], y3_s.at[d - 1], y3_r.at[d - 1], dev(dy=d))

    for d in (2, 1, 3):
        go(y3(d))
    for d in (1, 3, 2):
        y3(d).wait_recv()
    fin[...] = (((sy[gy] + ry[0]) + ry[1]) + ry[2]) * SCALE
    tiles = [fin[pl.ds(t * 8, 8), :] for t in range(6)]
    lane8 = lax.broadcasted_iota(jnp.int32, (8, 128), 1)

    def natural(mk):
        out = None
        for u in range(NSUB):
            at = u * 6 * U + mk * U
            turned = pltpu.roll(tiles[at // 128], (u * U - at) % 128, 1)
            out = turned if out is None else jnp.where(lane8 < u * U, out, turned)
        return out

    for m in range(2):
        by_dir = [natural(m * 3 + d) for d in range(3)]
        for k in range(3):
            want_dir = dir_ref[k]
            val = jnp.where(want_dir == 0, by_dir[0], jnp.where(want_dir == 1, by_dir[1], by_dir[2]))
            for part in range(2):
                out_ref[pl.ds((m * 3 + k) * 2 + part, 4, stride=12), :] = val[part * 4:part * 4 + 4]

    finish()


def group_scratch(n):
    vm = pltpu.VMEM
    return [
        vm((4, n, 2, 2, 16, 256), BF16), vm((3, n, 2, 2, 16, 256), BF16),
        vm((4, n, 2, 4, 16, 128), BF16), vm((3, n, 2, 4, 16, 128), BF16),
        vm((4, n, 2, 16, 128), F32), vm((3, n, 2, 16, 128), F32),
        vm((4, n, 2, 16, 128), F32), vm((3, n, 2, 16, 128), F32),
    ]


def per_device(vectors, links, momenta, shifts_dir):
    dma = lambda *n: pltpu.SemaphoreType.DMA(n)
    vm = pltpu.VMEM
    out = pl.pallas_call(
        kernel,
        out_shape=jax.ShapeDtypeStruct((48, 128), F32),
        in_specs=[
            pl.BlockSpec(memory_space=pl.ANY),
            pl.BlockSpec(memory_space=pl.ANY),
            pl.BlockSpec(memory_space=pltpu.SMEM),
            pl.BlockSpec(memory_space=pltpu.SMEM),
        ],
        out_specs=pl.BlockSpec(memory_space=pltpu.VMEM),
        scratch_shapes=[
            vm((6, 128, 1024), BF16),
            vm((288, 128), F32),
            vm((4, 1024, 256), BF16),
            vm((8, 6, 128, 128), BF16),
            vm((24, 2, 128, 128), BF16),
            vm((12, 2, 128, 128), BF16),
            vm((6, 2, 128, 128), BF16),
            vm((6, 128, 128), BF16),
            vm((6, 128, 128), BF16),
            vm((4, 48, 128), F32),
            vm((4, 48, 128), F32),
            vm((8, 128), F32),
            vm((8, 128), F32),
            vm((2, 768, 3072), BF16),
            vm((6, 2, 8, 16, 256), F32),
            vm((6, 2, 8, 16, 256), F32),
            vm((6, 2, 8, 16, 256), F32),
            *group_scratch(2), *group_scratch(1),
            vm((4, 48, 128), F32),
            vm((3, 48, 128), F32),
            vm((48, 128), F32),
            dma(NSUB), pltpu.SemaphoreType.DMA,
            dma(NSUB, 8), dma(NSUB, 8), dma(4), dma(4),
            dma(NSUB), dma(NSUB), dma(NSUB), dma(NSUB), dma(6), dma(6),
            *[dma(2, 3) for _ in range(8)], dma(3), dma(3),
        ],
        compiler_params=pltpu.CompilerParams(
            collective_id=0, has_side_effects=True, vmem_limit_bytes=56 * 1024 * 1024
        ),
        name="elementals",
    )(vectors.reshape(6, 128, 1024), links.reshape(288, 128), momenta, shifts_dir)
    return out.reshape(4, 2, 3, 2, 128)


def solution(mesh):
    in_specs = (P(None, None, "vert", "gx", "gy"), P(None, None, None, None, "gx", "gy"), P(), P())
    out_specs = P(("gx", "gy"), None, None, None, "vert")
    return jax.shard_map(
        per_device, mesh=mesh, in_specs=in_specs, out_specs=out_specs, check_vma=False
    )
```

```python
import math

import jax
import jax.numpy as jnp
from jax import lax
from jax.experimental import pallas as pl
from jax.experimental.pallas import tpu as pltpu
from jax.sharding import PartitionSpec as P

MESH = pl.DeviceIdType.MESH
F32 = jnp.float32
BF16 = jnp.bfloat16

NSUB = 4
AHEAD = 2
U = 128 // NSUB
NT = (((1,), (1,)), ((), ()))
SCALE = 1.0 / math.sqrt(3.0 * 16 * 64 * 64)
PEERS_X = [(d, dc) for d in (2, 1, 3, 0) for dc in (0, 1) if d or dc]


def kernel(
    vec_hbm, links_hbm, mom_hbm, dir_hbm, out_ref,
    mom_ref, dir_ref, small_sem,
    vbuf, lbuf, perm, sbuf, lhs, neg, xh, hs, hr, lsend, ul, ct, st, wt_a, wt_b, wt_c,
    ek, ex, er, sz_a, rz_a, sx_a, rx_a, sz2_a, rz2_a, sx2_a, rx2_a,
    sz_b, rz_b, sx_b, rx_b, sz2_b, rz2_b, sx2_b, rx2_b, sy, ry, fin,
    vsem, lsem, a_s, a_r, l_s, l_r, xh_s, xh_r, yh_s, yh_r, c_s, c_r,
    z1_s, z1_r, x1_s, x1_r, z2_s, z2_r, x2_s, x2_r, y3_s, y3_r,
):
    gx, gy, hi = lax.axis_index("gx"), lax.axis_index("gy"), lax.axis_index("vert")
    z, lo, c = gx // 4, (gx // 2) % 2, gx % 2
    x = hi * 2 + lo
    e = x * 2 + c
    layer = lo * 2 + c

    def dev(dz=0, dy=0, dx=0, dc=0):
        tx = (x + dx) % 4
        tz = (z + dz) % 4
        tc = (c + dc) % 2
        return (tz * 4 + (tx % 2) * 2 + tc, (gy + dy) % 4, tx // 2)

    pending = []

    def go(copy):
        copy.start()
        pending.append(copy)

    def finish():
        for copy in pending:
            copy.wait_send()

    def remote(src, dst, s, r, where):
        return pltpu.make_async_remote_copy(
            src_ref=src, dst_ref=dst, send_sem=s, recv_sem=r, device_id=where, device_id_type=MESH
        )

    barrier = pltpu.get_barrier_semaphore()
    peers = [dev(dx=d, dc=dc) for d, dc in PEERS_X]
    peers += [dev(dz=d) for d in (1, 2, 3)] + [dev(dy=d) for d in (1, 2, 3)]
    for p in peers:
        pl.semaphore_signal(barrier, inc=1, device_id=p, device_id_type=MESH)

    small = [
        pltpu.make_async_copy(mom_hbm, mom_ref, small_sem.at[0]),
        pltpu.make_async_copy(dir_hbm, dir_ref, small_sem.at[1]),
    ]
    for cp in small:
        cp.start()
    loads = []
    for u in range(NSUB):
        cp = pltpu.make_async_copy(
            vec_hbm.at[:, pl.ds(u * U, U), :], vbuf.at[:, pl.ds(u * U, U), :], vsem.at[u]
        )
        cp.start()
        loads.append(cp)
    lcopy = pltpu.make_async_copy(links_hbm, lbuf, lsem)
    lcopy.start()

    site = lax.broadcasted_iota(jnp.int32, (1024, 256), 0)
    col = lax.broadcasted_iota(jnp.int32, (1024, 256), 1)
    core_of = jnp.where(col < 128, c, 1 - c)
    lane = col % 128
    want = (lane // 8) * 64 + lane % 8 + core_of * 8
    for d in range(4):
        q = (x + d) % 4
        perm[d] = jnp.where(site == want + q * 16, 1.0, 0.0).astype(BF16)

    for cp in small:
        cp.wait()

    row = lax.broadcasted_iota(jnp.int32, (8, 128), 0)
    ln = lax.broadcasted_iota(jnp.int32, (8, 128), 1)
    first = row < 4
    px = jnp.where(first, mom_ref[0, 0], mom_ref[1, 0])
    py = jnp.where(first, mom_ref[0, 1], mom_ref[1, 1])
    pz = jnp.where(first, mom_ref[0, 2], mom_ref[1, 2])
    turn = (
        4 * ((px * (z * 4 + row % 4)) & 15)
        + ((py * (gy * 16 + ln // 8)) & 63)
        + ((pz * (e * 8 + ln % 8)) & 63)
    )
    angle = (2.0 * math.pi) * (turn.astype(F32) * (1.0 / 64.0))
    ct[...] = jnp.cos(angle)
    st[...] = jnp.sin(angle)

    pl.semaphore_wait(barrier, len(peers))

    def a2a(u, d, dc):
        return remote(
            sbuf.at[d * 2 + dc, :, pl.ds(u * U, U), :],
            lhs.at[pl.ds(layer * 6, 6), hi, pl.ds(u * U, U), :],
            a_s.at[u, d * 2 + dc], a_r.at[u, d * 2 + dc], dev(dx=d, dc=dc),
        )

    def a2a_in(u, d, dc):
        sx_ = (x - d + 4) % 4
        slayer = (sx_ % 2) * 2 + (c + dc) % 2
        return remote(
            sbuf.at[d * 2 + dc, :, pl.ds(u * U, U), :],
            lhs.at[pl.ds(slayer * 6, 6), sx_ // 2, pl.ds(u * U, U), :],
            a_s.at[u, d * 2 + dc], a_r.at[u, d * 2 + dc], dev(dx=d, dc=dc),
        )

    def move(u):
        loads[u].wait()
        mine = vbuf[:, u * U:(u + 1) * U, :].reshape(6 * U, 1024)
        for d in (2, 1, 3, 0):
            moved = jnp.dot(mine, perm[d], preferred_element_type=F32).astype(BF16)
            for dc in (0, 1):
                part = moved[:, dc * 128:(dc + 1) * 128].reshape(6, U, 128)
                if d or dc:
                    sbuf[d * 2 + dc, :, u * U:(u + 1) * U, :] = part
                else:
                    lhs[pl.ds(layer * 6, 6), hi, u * U:(u + 1) * U, :] = part
                if u < AHEAD and (d or dc):
                    go(a2a(u, d, dc))

    def link_copy(i, dc, slayer):
        tx = hi * 2 + (lo + i) % 2
        return remote(
            lsend.at[i * 2 + dc], ul.at[slayer], l_s.at[i * 2 + dc], l_r.at[i * 2 + dc],
            (z * 4 + (tx % 2) * 2 + (c + dc) % 2, gy, hi),
        )

    LINKS = [(0, 1), (1, 0), (1, 1)]

    def move_links():
        lcopy.wait()
        rows = [lbuf[pl.ds(t, 36, stride=8), :] for t in range(8)]
        link = jnp.concatenate(rows, axis=1)
        link = jnp.concatenate([link, jnp.zeros((12, 1024), F32)], axis=0)
        part0 = link.astype(BF16)
        rest = link - part0.astype(F32)
        part1 = rest.astype(BF16)
        part2 = (rest - part1.astype(F32)).astype(BF16)
        parts = jnp.concatenate([part0, part1, part2], axis=0)
        for i in range(2):
            slot = 0 if i == 0 else 1 + 2 * lo
            got = jnp.dot(parts, perm[slot], preferred_element_type=F32)
            total = (got[0:48] + got[48:96]) + got[96:144]
            for dc in (0, 1):
                piece = total[:, dc * 128:(dc + 1) * 128]
                if i or dc:
                    lsend[i * 2 + dc] = piece
                else:
                    ul[layer] = piece
        for i, dc in LINKS:
            go(link_copy(i, dc, layer))

    move(0)
    move_links()
    for u in range(1, NSUB):
        move(u)
    for i, dc in LINKS:
        link_copy(i, dc, ((lo + i) % 2) * 2 + (c + dc) % 2).wait_recv()

    lane16 = lax.broadcasted_iota(jnp.int32, (16, 128), 1)

    def transport(l, d, f):
        out = []
        for r in range(3):
            are = aim = None
            for k in range(3):
                ure = ul[l, pl.ds(((d * 2 + 0) * 3 + r) * 3 + k, 1), :]
                uim = ul[l, pl.ds(((d * 2 + 1) * 3 + r) * 3 + k, 1), :]
                tre = ure * f[k] - uim * f[3 + k]
                tim = ure * f[3 + k] + uim * f[k]
                are = tre if are is None else are + tre
                aim = tim if aim is None else aim + tim
            out.append((are, aim))
        return out

    WT = ((wt_a, 0, 384), (wt_b, 384, 128), (wt_c, 512, 256))

    def put(l, d, v, u, r0, f):
        for m in range(2):
            cs = ct[pl.ds(m * 4 + l, 1), :]
            sn = st[pl.ds(m * 4 + l, 1), :]
            at = u * 6 * U + (d * 2 + m) * U
            wt, base = next((w, b) for w, b, n in WT if b <= at < b + n)
            cols = pl.ds(pl.multiple_of(at - base + r0, 16), 16)
            for r in range(3):
                fre, fim = f[r]
                wre = (fre * cs + fim * sn).astype(BF16)
                wim = (fim * cs - fre * sn).astype(BF16)
                wt[v, cols, pl.ds((l * 6 + r) * 128, 128)] = wre
                wt[v, cols, pl.ds((l * 6 + 3 + r) * 128, 128)] = wim

    def xh_copy(u):
        return remote(
            lhs.at[pl.ds(0, 6), :, pl.ds(u * U, U), :], xh.at[:, :, pl.ds(u * U, U), :],
            xh_s.at[u], xh_r.at[u], dev(dz=3),
        )

    def yh_copy(u):
        return remote(
            hs.at[:, pl.ds(u * U, U), :], hr.at[:, pl.ds(u * U, U), :],
            yh_s.at[u], yh_r.at[u], dev(dy=3),
        )

    CH = U // 16

    def pack(u):
        def body(j, carry):
            rows = pl.ds(pl.multiple_of(u * U + j * 16, 16), 16)
            for i in range(6):
                acc = lhs[i, 0, rows, :].astype(F32)
                for s in range(1, 8):
                    v, l = s // 4, s % 4
                    piece = pltpu.roll(lhs[l * 6 + i, v, rows, :].astype(F32), 8 * s, 1)
                    acc = jnp.where(lane16 < 8 * s, acc, piece)
                hs[i, rows, :] = acc.astype(BF16)
            for l in range(4):
                for r in range(3):
                    for v in range(2):
                        neg[l * 3 + r, v, rows, :] = -lhs[l * 6 + 3 + r, v, rows, :]
            return carry

        lax.fori_loop(0, CH, body, 0)

    def free_chunk(u, j):
        v = j // CH
        r0 = (j % CH) * 16
        rows = pl.ds(pl.multiple_of(u * U + r0, 16), 16)
        for l in range(4):
            f = [lhs[l * 6 + i, v, rows, :].astype(F32) for i in range(6)]
            put(l, 0, v, u, r0, [(f[r], f[3 + r]) for r in range(3)])
            if l < 3:
                f = [lhs[l * 6 + 6 + i, v, rows, :].astype(F32) for i in range(6)]
                put(l, 1, v, u, r0, transport(l, 0, f))

    def free(u):
        def body(j, carry):
            free_chunk(u, j)
            return carry

        lax.fori_loop(0, 2 * CH, body, 0)

    def halo_chunk(u, j):
        r0 = j * 16
        rows = pl.ds(pl.multiple_of(u * U + r0, 16), 16)
        for v in range(2):
            f = [xh[i, v, rows, :].astype(F32) for i in range(6)]
            put(3, 1, v, u, r0, transport(3, 0, f))
            for l in range(4):
                f = []
                for i in range(6):
                    here = pltpu.roll(lhs[l * 6 + i, v, rows, :].astype(F32), 120, 1)
                    shift = (120 - 8 * (v * 4 + l)) % 128
                    edge = hr[i, rows, :].astype(F32)
                    edge = pltpu.roll(edge, shift, 1) if shift else edge
                    f.append(jnp.where(lane16 < 120, here, edge))
                put(l, 2, v, u, r0, transport(l, 1, f))

    def halo_wait(u):
        xh_copy(u).wait_recv()
        yh_copy(u).wait_recv()

    def halo(u):
        def body(j, carry):
            halo_chunk(u, j)
            return carry

        lax.fori_loop(0, CH, body, 0)

    def core_copy(j):
        return remote(ex.at[j], er.at[j], c_s.at[j], c_r.at[j], dev(dc=1))

    def product(j, first, last):
        count = (last - first) * U
        sub = slice(first * U, last * U)
        if isinstance(j, int) and j >= 3:
            wt, base, _ = WT[1 if j == 3 else 2]
            right = wt[:, j * 128 - base:j * 128 - base + 128, :].reshape(256, 3072)
        else:
            right = wt_a[:, pl.ds(pl.multiple_of(j * 128, 128), 128), :].reshape(256, 3072)
        re = [lhs[t, :, sub, :].reshape(2 * count, 128) for t in range(24)]
        im = []
        for l in range(4):
            im += [neg[l * 3 + r, :, sub, :].reshape(2 * count, 128) for r in range(3)]
            im += [lhs[l * 6 + r, :, sub, :].reshape(2 * count, 128) for r in range(3)]
        left = jnp.concatenate([jnp.concatenate(re, axis=1), jnp.concatenate(im, axis=1)], axis=0)
        prod = lax.dot_general(left, right, NT, preferred_element_type=F32)
        groups = prod.reshape(2, 2, count // 32, 2, 16, 256)
        for part in range(2):
            for v in range(2):
                even, odd = groups[part, v, :, 0], groups[part, v, :, 1]
                at = slice(v * 4 + first * U // 32, v * 4 + last * U // 32)
                ek[j, part, at] = jnp.where(c == 0, even, odd)
                ex[j, part, at] = jnp.where(c == 0, odd, even)

    class Group:
        def __init__(self, n, jz, jx, refs):
            self.n, self.jz, self.jx = n, jz, jx
            (self.sz, self.rz, self.sx, self.rx, self.sz2, self.rz2, self.sx2, self.rx2) = refs

        def z1(self, d):
            n = self.n
            return remote(self.sz.at[(z + d) % 4], self.rz.at[d - 1], z1_s.at[n, d - 1], z1_r.at[n, d - 1], dev(dz=d))

        def x1(self, d):
            n = self.n
            return remote(self.sx.at[(x + d) % 4], self.rx.at[d - 1], x1_s.at[n, d - 1], x1_r.at[n, d - 1], dev(dx=d))

        def z2(self, d):
            n = self.n
            return remote(self.sz2.at[(z + d) % 4], self.rz2.at[d - 1], z2_s.at[n, d - 1], z2_r.at[n, d - 1], dev(dz=d))

        def x2(self, d):
            n = self.n
            return remote(self.sx2.at[(x + d) % 4], self.rx2.at[d - 1], x2_s.at[n, d - 1], x2_r.at[n, d - 1], dev(dx=d))

        def first(self):
            for j in sorted({j for j, _ in self.jz + self.jx}):
                core_copy(j).wait_recv()
            for k, (j, part) in enumerate(self.jz):
                total = ek[j, part] + er[j, part]
                ek[j, part] = total
                for t in range(4):
                    self.sz[t, k] = total[2 * t:2 * t + 2].astype(BF16)
            for d in (2, 1, 3):
                go(self.z1(d))
            for k, (j, part) in enumerate(self.jx):
                total = ek[j, part] + er[j, part]
                ek[j, part] = total
                four = total.reshape(4, 2, 16, 256)
                for t in range(4):
                    half = four[:, t % 2][:, :, (t // 2) * 128:(t // 2) * 128 + 128]
                    self.sx[t, k] = half.astype(BF16)
            for d in (2, 1, 3):
                go(self.x1(d))

        def second(self):
            for d in (1, 3, 2):
                self.z1(d).wait_recv()
            for k, (j, part) in enumerate(self.jz):
                total = ek[j, part, pl.ds(z * 2, 2)]
                for d in range(3):
                    total = total + self.rz[d, k].astype(F32)
                for t in range(4):
                    self.sx2[t, k] = total[t % 2, :, (t // 2) * 128:(t // 2) * 128 + 128]
            for d in (2, 1, 3):
                go(self.x2(d))
            for d in (1, 3, 2):
                self.x1(d).wait_recv()
            for k, (j, part) in enumerate(self.jx):
                for t in range(4):
                    total = ek[j, part, t * 2 + lo, :, pl.ds(pl.multiple_of(hi * 128, 128), 128)]
                    for d in range(3):
                        total = total + self.rx[d, k, t].astype(F32)
                    self.sz2[t, k] = total
            for d in (2, 1, 3):
                go(self.z2(d))

        def third(self):
            for js, own, sent, got, copy in (
                (self.jz, x, self.sx2, self.rx2, self.x2), (self.jx, z, self.sz2, self.rz2, self.z2)
            ):
                for d in (1, 3, 2):
                    copy(d).wait_recv()
                for k, (j, part) in enumerate(js):
                    total = sent[own, k]
                    for d in range(3):
                        total = total + got[d, k]
                    for t in range(4):
                        sy[t, pl.ds((j * 2 + part) * 4, 4), :] = total[t * 4:t * 4 + 4]

    early = Group(
        0, ((0, 0), (0, 1), (1, 0), (1, 1)), ((2, 0), (2, 1), (3, 0), (3, 1)),
        (sz_a, rz_a, sx_a, rx_a, sz2_a, rz2_a, sx2_a, rx2_a),
    )
    late = Group(1, ((4, 0), (4, 1)), ((5, 0), (5, 1)), (sz_b, rz_b, sx_b, rx_b, sz2_b, rz2_b, sx2_b, rx2_b))

    for u in range(NSUB):
        for d, dc in PEERS_X:
            a2a_in(u, d, dc).wait_recv()
        go(xh_copy(u))
        pack(u)
        go(yh_copy(u))
        if u + AHEAD < NSUB:
            for d, dc in PEERS_X:
                go(a2a(u + AHEAD, d, dc))
        if u < 3:
            free(u)
            if u:
                halo_wait(u - 1)
                halo(u - 1)
            if u == 2:
                def block(j, carry):
                    product(j, 0, 2)
                    return carry

                lax.fori_loop(0, 3, block, 0)
        else:
            halo_wait(2)

            def both(j, carry):
                product(j, 2, 4)
                halo_chunk(2, j)
                free_chunk(3, j)
                core_copy(j).start()
                return carry

            lax.fori_loop(0, 2, both, 0)
            product(2, 2, 4)
            free_chunk(3, 2)
            core_copy(2).start()
            product(3, 0, 4)
            free_chunk(3, 3)
            core_copy(3).start()
            product(4, 0, 4)
            core_copy(4).start()
            halo_wait(3)
            halo(3)
    early.first()
    product(5, 0, 4)
    core_copy(5).start()
    late.first()
    early.second()
    late.second()
    early.third()
    late.third()
    pending.extend(core_copy(j) for j in range(6))

    def y3(d):
        return remote(sy.at[(gy + d) % 4], ry.at[d - 1], y3_s.at[d - 1], y3_r.at[d - 1], dev(dy=d))

    for d in (2, 1, 3):
        go(y3(d))
    for d in (1, 3, 2):
        y3(d).wait_recv()
    fin[...] = (((sy[gy] + ry[0]) + ry[1]) + ry[2]) * SCALE
    tiles = [fin[pl.ds(t * 8, 8), :] for t in range(6)]
    lane8 = lax.broadcasted_iota(jnp.int32, (8, 128), 1)

    def natural(m, d):
        out = None
        for u in range(NSUB):
            at = u * 6 * U + (d * 2 + m) * U
            turned = pltpu.roll(tiles[at // 128], (u * U - at) % 128, 1)
            out = turned if out is None else jnp.where(lane8 < u * U, out, turned)
        return out

    for m in range(2):
        by_dir = [natural(m, d) for d in range(3)]
        for k in range(3):
            want_dir = dir_ref[k]
            val = jnp.where(want_dir == 0, by_dir[0], jnp.where(want_dir == 1, by_dir[1], by_dir[2]))
            for part in range(2):
                out_ref[pl.ds((m * 3 + k) * 2 + part, 4, stride=12), :] = val[part * 4:part * 4 + 4]

    finish()


def group_scratch(n):
    vm = pltpu.VMEM
    return [
        vm((4, n, 2, 16, 256), BF16), vm((3, n, 2, 16, 256), BF16),
        vm((4, n, 4, 16, 128), BF16), vm((3, n, 4, 16, 128), BF16),
        vm((4, n, 16, 128), F32), vm((3, n, 16, 128), F32),
        vm((4, n, 16, 128), F32), vm((3, n, 16, 128), F32),
    ]


def per_device(vectors, links, momenta, shifts_dir):
    dma = lambda *n: pltpu.SemaphoreType.DMA(n)
    vm = pltpu.VMEM
    out = pl.pallas_call(
        kernel,
        out_shape=jax.ShapeDtypeStruct((48, 128), F32),
        in_specs=[
            pl.BlockSpec(memory_space=pl.ANY),
            pl.BlockSpec(memory_space=pl.ANY),
            pl.BlockSpec(memory_space=pl.ANY),
            pl.BlockSpec(memory_space=pl.ANY),
        ],
        out_specs=pl.BlockSpec(memory_space=pltpu.VMEM),
        scratch_shapes=[
            pltpu.SMEM((2, 3), jnp.int32), pltpu.SMEM((3,), jnp.int32), dma(2),
            vm((6, 128, 1024), BF16),
            vm((288, 128), F32),
            vm((4, 1024, 256), BF16),
            vm((8, 6, 128, 128), BF16),
            vm((24, 2, 128, 128), BF16),
            vm((12, 2, 128, 128), BF16),
            vm((6, 2, 128, 128), BF16),
            vm((6, 128, 128), BF16),
            vm((6, 128, 128), BF16),
            vm((4, 48, 128), F32),
            vm((4, 48, 128), F32),
            vm((8, 128), F32),
            vm((8, 128), F32),
            vm((2, 384, 3072), BF16),
            vm((2, 128, 3072), BF16),
            vm((2, 256, 3072), BF16),
            vm((6, 2, 8, 16, 256), F32),
            vm((6, 2, 8, 16, 256), F32),
            vm((6, 2, 8, 16, 256), F32),
            *group_scratch(4), *group_scratch(2),
            vm((4, 48, 128), F32),
            vm((3, 48, 128), F32),
            vm((48, 128), F32),
            dma(NSUB), pltpu.SemaphoreType.DMA,
            dma(NSUB, 8), dma(NSUB, 8), dma(4), dma(4),
            dma(NSUB), dma(NSUB), dma(NSUB), dma(NSUB), dma(6), dma(6),
            *[dma(2, 3) for _ in range(8)], dma(3), dma(3),
        ],
        compiler_params=pltpu.CompilerParams(
            collective_id=0, has_side_effects=True, vmem_limit_bytes=56 * 1024 * 1024
        ),
        name="elementals",
    )(vectors.reshape(6, 128, 1024), links.reshape(288, 128), momenta, shifts_dir)
    return out.reshape(4, 2, 3, 2, 128)


def solution(mesh):
    in_specs = (P(None, None, "vert", "gx", "gy"), P(None, None, None, None, "gx", "gy"), P(), P())
    out_specs = P(("gx", "gy"), None, None, None, "vert")
    return jax.shard_map(
        per_device, mesh=mesh, in_specs=in_specs, out_specs=out_specs, check_vma=False
    )
```
